128 devices in a mesh: samp: 16 (over x, z_hi, core), par: 8 (over z_lo, y).
Axes of the slice: x: 4, y: 4, z: 4 (z_hi: 2, z_lo: 2; z = z_hi * 2 + z_lo), core: 2. Of those that a mesh axis runs over, the one named last changes fastest.
Arguments:
- log_derivs: float32 [256, 262144], P('samp', 'par'), as said below
Outputs:
- kernel: float32 [256, 256], P('samp', 'par')
Inputs may be any that keep to these rules, and one draw needn't show every extreme that they name: `log_derivs`: real values; rows differ in scale.
All inputs are finite; a program needn't handle non-finite values.
Results may differ from the reference program's by a relative error of at most 0.00005.
Values sent between devices are 32-bit elements; how exact they have to be, the bound alone decides.
A program may use at most 64 MiB of HBM per device.

```python
import math
import jax
import jax.numpy as jnp
from jax import lax

PARAMS = 262144
SAMPLES = 256


def draw_log_derivs(key, part):
    key = jax.random.fold_in(key, 11)
    keys = jax.random.split(key, 7)
    freqs = jax.random.uniform(keys[0], (PARAMS,), jnp.float32, 0.5, 6.0)
    phases = jax.random.uniform(keys[1], (PARAMS,), jnp.float32, -math.pi, math.pi)
    column_scale = jnp.exp(jax.random.uniform(keys[2], (PARAMS,), jnp.float32, 0.0, math.log(10.0)))
    offsets = 0.5 * jax.random.normal(keys[3], (PARAMS,), jnp.float32)
    coords = jax.random.uniform(keys[4], (SAMPLES,), jnp.float32, -1.0, 1.0)
    scale = jnp.sqrt(SAMPLES / (PARAMS * 84.0))
    rising = 1.0 + 2.0 * jnp.arange(SAMPLES, dtype=jnp.float32) / SAMPLES
    row_scale = rising * jax.random.uniform(keys[5], (SAMPLES,), jnp.float32, 0.8, 1.25)
    noise = jax.random.normal(keys[6], (SAMPLES, PARAMS), jnp.float32)
    waves = jnp.cos(coords[:, None] * freqs[None, :] + phases[None, :])
    values = (waves + offsets[None, :] + 0.4 * noise) * column_scale[None, :]
    return (row_scale[:, None] * values * scale).astype(jnp.float32)


def setup_inputs(seed: int = 0) -> dict:
    splits = jax.random.split(jax.random.key(seed), 2)
    return {
        "log_derivs": draw_log_derivs(jax.random.fold_in(splits[1], 71), 0),
    }


diag_shift = 0.01


def reference(log_derivs):
    column_mean = jnp.sum(log_derivs, axis=0) / SAMPLES
    centered = log_derivs - column_mean[None, :]
    gram = jnp.dot(centered, centered.T, precision=lax.Precision.HIGHEST, preferred_element_type=jnp.float32)
    identity = jnp.eye(SAMPLES, dtype=jnp.float32)
    return gram / SAMPLES + diag_shift * identity
```

```python
import jax
import jax.numpy as jnp
from jax import lax
from jax.experimental import pallas as pl
from jax.experimental.pallas import tpu as pltpu
from jax.sharding import PartitionSpec as P

diag_shift = 0.01
MESH = pl.DeviceIdType.MESH

ROWS = 16
SAMP = 16
PAR = 8
TOTAL = ROWS * SAMP
CHUNKS = 4

PARTNERS = [
    (2, 1, 0), (2, 1, 1), (1, 1, 0), (3, 1, 1), (1, 1, 1), (3, 1, 0), (2, 0, 0), (2, 0, 1),
    (0, 1, 0), (0, 1, 1), (1, 0, 0), (3, 0, 1), (1, 0, 1), (3, 0, 0), (0, 0, 1),
]


def samp_partner(samp, delta):
    x, z, c = samp // 4, (samp // 2) % 2, samp % 2
    return (((x + delta[0]) % 4) * 2 + (z + delta[1]) % 2) * 2 + (c + delta[2]) % 2


def kernel(x_ref, o_ref, full, acc, pack, parts, local_sem, a_send, a_recv, r_send, r_recv):
    samp, par = lax.axis_index("samp"), lax.axis_index("par")
    share = full.shape[1]
    width = share // CHUNKS

    barrier = pltpu.get_barrier_semaphore()
    for i in range(1, SAMP):
        pl.semaphore_signal(barrier, inc=1, device_id=((samp + i) % SAMP, par), device_id_type=MESH)
    for i in range(1, PAR):
        pl.semaphore_signal(barrier, inc=1, device_id=(samp, (par + i) % PAR), device_id_type=MESH)

    own = pl.ds(pl.multiple_of(samp * ROWS, ROWS), ROWS)
    keep = pltpu.make_async_copy(
        x_ref.at[:, pl.ds(pl.multiple_of(samp * share, share), share)], full.at[own, :], local_sem
    )
    keep.start()
    acc[...] = jnp.zeros_like(acc)
    pl.semaphore_wait(barrier, SAMP + PAR - 2)

    def send_chunk(k, carry):
        for delta in PARTNERS:
            to = samp_partner(samp, delta)
            pltpu.make_async_remote_copy(
                src_ref=x_ref.at[:, pl.ds(pl.multiple_of(to * share + k * width, width), width)],
                dst_ref=full.at[own, pl.ds(pl.multiple_of(k * width, width), width)],
                send_sem=a_send,
                recv_sem=a_recv.at[k],
                device_id=(to, par),
                device_id_type=MESH,
            ).start()
        return carry

    lax.fori_loop(0, CHUNKS, send_chunk, 0)
    keep.wait()

    def gram_chunk(k, carry):
        cols = pl.ds(pl.multiple_of(k * width, width), width)
        got = full.at[pl.ds(0, TOTAL - ROWS), cols]
        pltpu.make_async_copy(got, got, a_recv.at[k]).wait()
        block = full[:, cols]
        block = block - jnp.sum(block, axis=0, keepdims=True) / TOTAL
        high = block.astype(jnp.bfloat16)
        low = (block - high.astype(jnp.float32)).astype(jnp.bfloat16)

        def dot(a, b):
            return lax.dot_general(a, b, (((1,), (1,)), ((), ())), preferred_element_type=jnp.float32)

        acc[...] += dot(high, high) + (dot(high, low) + dot(low, high))
        return carry

    lax.fori_loop(0, CHUNKS, gram_chunk, 0)

    lane = lax.broadcasted_iota(jnp.int32, (8, 128), 1)
    top = lax.broadcasted_iota(jnp.int32, (8, 128), 0) < 4
    even, left = (lane // 32) % 2 == 0, lane < 64

    def pack_rows(t, carry):
        for half in range(2):
            v = [
                acc[pl.ds(pl.multiple_of(t * 32 + i * 8, 8), 8), half * 128 : half * 128 + 128] for i in range(4)
            ]
            u = []
            for h in range(2):
                u.append(jnp.where(top, v[h], pltpu.roll(v[2 + h], 4, 0)))
                u.append(jnp.where(top, pltpu.roll(v[h], 4, 0), v[2 + h]))
            w = [[None, None], [None, None]]
            for a in range(2):
                w[a][0] = jnp.where(even, u[2 * a], pltpu.roll(u[2 * a + 1], 32, 1))
                w[a][1] = jnp.where(even, pltpu.roll(u[2 * a], 96, 1), u[2 * a + 1])
            for y0 in range(2):
                for b in range(2):
                    if b == 0:
                        tile = jnp.where(left, w[0][y0], pltpu.roll(w[1][y0], 64, 1))
                    else:
                        tile = jnp.where(left, pltpu.roll(w[0][y0], 64, 1), w[1][y0])
                    place = t * 8 + half * 4 + 2 * b + y0
                    pack[0, place] = tile[0:4]
                    pack[1, place] = tile[4:8]
        return carry

    lax.fori_loop(0, SAMP // 2, pack_rows, 0)

    me = samp * PAR + par

    def send_tile(i, carry):
        k = SAMP * PAR - 1 - i
        to_s, to_p = (samp + k // PAR) % SAMP, (par + k % PAR) % PAR
        pltpu.make_async_remote_copy(
            src_ref=pack.at[to_s % 2, (to_s // 2) * PAR + to_p],
            dst_ref=parts.at[me],
            send_sem=r_send,
            recv_sem=r_recv,
            device_id=(to_s, to_p),
            device_id_type=MESH,
        ).start()
        return carry

    lax.fori_loop(0, SAMP * PAR - 1, send_tile, 0)
    parts[me] = pack[samp % 2, (samp // 2) * PAR + par]

    got = parts.at[pl.ds(0, SAMP * PAR - 1)]
    pltpu.make_async_copy(got, got, r_recv).wait()
    tile = jnp.sum(parts[...], axis=0)
    row = samp * ROWS + lax.broadcasted_iota(jnp.int32, (4, 32), 0)
    col = par * 32 + lax.broadcasted_iota(jnp.int32, (4, 32), 1)
    for g in range(4):
        shift = jnp.where(row + 4 * g == col, diag_shift, 0.0)
        o_ref[4 * g : 4 * g + 4, :] = tile[:, 32 * g : 32 * g + 32] / TOTAL + shift

    pltpu.make_async_copy(got, got, r_send).wait()
    sent = full.at[pl.ds(0, TOTAL - ROWS), :]
    pltpu.make_async_copy(sent, sent, a_send).wait()


def body(log_derivs):
    share = log_derivs.shape[1] // SAMP
    return pl.pallas_call(
        kernel,
        out_shape=jax.ShapeDtypeStruct((ROWS, TOTAL // PAR), jnp.float32),
        in_specs=[pl.BlockSpec(memory_space=pl.ANY)],
        out_specs=pl.BlockSpec(memory_space=pltpu.VMEM),
        scratch_shapes=[
            pltpu.VMEM((TOTAL, share), jnp.float32),
            pltpu.VMEM((TOTAL, TOTAL), jnp.float32),
            pltpu.VMEM((2, SAMP * PAR // 2, 4, 128), jnp.float32),
            pltpu.VMEM((SAMP * PAR, 4, 128), jnp.float32),
            pltpu.SemaphoreType.DMA,
            pltpu.SemaphoreType.DMA,
            pltpu.SemaphoreType.DMA((CHUNKS,)),
            pltpu.SemaphoreType.DMA,
            pltpu.SemaphoreType.DMA,
        ],
        compiler_params=pltpu.CompilerParams(
            collective_id=0, has_side_effects=True, vmem_limit_bytes=48 * 1024 * 1024
        ),
        cost_estimate=pl.CostEstimate(flops=3 * 2 * TOTAL * TOTAL * share, bytes_accessed=2 << 20, transcendentals=0),
        name="sample_kernel",
    )(log_derivs)


def solution(mesh):
    return jax.shard_map(
        body,
        mesh=mesh,
        in_specs=(P("samp", "par"),),
        out_specs=P("samp", "par"),
        check_vma=False,
    )
```

```python
import jax
import jax.numpy as jnp
from jax import lax
from jax.experimental import pallas as pl
from jax.experimental.pallas import tpu as pltpu
from jax.sharding import PartitionSpec as P

diag_shift = 0.01
MESH = pl.DeviceIdType.MESH

ROWS = 16
SAMP = 16
PAR = 8
TOTAL = ROWS * SAMP
CHUNKS = 4

PARTNERS = [
    (2, 1, 0), (2, 1, 1), (1, 1, 0), (3, 1, 1), (1, 1, 1), (3, 1, 0), (2, 0, 0), (2, 0, 1),
    (0, 1, 0), (0, 1, 1), (1, 0, 0), (3, 0, 1), (1, 0, 1), (3, 0, 0), (0, 0, 1),
]


def samp_partner(samp, delta):
    x, z, c = samp // 4, (samp // 2) % 2, samp % 2
    return (((x + delta[0]) % 4) * 2 + (z + delta[1]) % 2) * 2 + (c + delta[2]) % 2


def ring_distance(delta):
    return min(delta, 4 - delta)


OTHERS = sorted(
    [(a, b, c, d) for a in range(4) for b in range(4) for c in range(4) for d in range(2) if a + b + c + d > 0],
    key=lambda k: -3 * sum(ring_distance(i) for i in k[:3]) - k[3],
)


def kernel(x_ref, o_ref, full, acc, pack, parts, local_sem, a_send, a_recv, r_send, r_recv):
    samp, par = lax.axis_index("samp"), lax.axis_index("par")
    share = full.shape[1]
    width = share // CHUNKS

    barrier = pltpu.get_barrier_semaphore()
    for i in range(1, SAMP):
        pl.semaphore_signal(barrier, inc=1, device_id=((samp + i) % SAMP, par), device_id_type=MESH)
    for i in range(1, PAR):
        pl.semaphore_signal(barrier, inc=1, device_id=(samp, (par + i) % PAR), device_id_type=MESH)

    own = pl.ds(pl.multiple_of(samp * ROWS, ROWS), ROWS)
    keep = pltpu.make_async_copy(
        x_ref.at[:, pl.ds(pl.multiple_of(samp * share, share), share)], full.at[own, :], local_sem
    )
    keep.start()
    acc[...] = jnp.zeros_like(acc)
    pl.semaphore_wait(barrier, SAMP + PAR - 2)

    def send_chunk(k, carry):
        for delta in PARTNERS:
            to = samp_partner(samp, delta)
            pltpu.make_async_remote_copy(
                src_ref=x_ref.at[:, pl.ds(pl.multiple_of(to * share + k * width, width), width)],
                dst_ref=full.at[own, pl.ds(pl.multiple_of(k * width, width), width)],
                send_sem=a_send,
                recv_sem=a_recv.at[k],
                device_id=(to, par),
                device_id_type=MESH,
            ).start()
        return carry

    lax.fori_loop(0, CHUNKS, send_chunk, 0)
    keep.wait()

    def gram_chunk(k, carry):
        cols = pl.ds(pl.multiple_of(k * width, width), width)
        got = full.at[pl.ds(0, TOTAL - ROWS), cols]
        pltpu.make_async_copy(got, got, a_recv.at[k]).wait()
        block = full[:, cols]
        block = block - jnp.sum(block, axis=0, keepdims=True) / TOTAL
        high = block.astype(jnp.bfloat16)
        low = (block - high.astype(jnp.float32)).astype(jnp.bfloat16)

        def dot(a, b):
            return lax.dot_general(a, b, (((1,), (1,)), ((), ())), preferred_element_type=jnp.float32)

        acc[...] += dot(high, high) + (dot(high, low) + dot(low, high))
        return carry

    lax.fori_loop(0, CHUNKS, gram_chunk, 0)

    lane = lax.broadcasted_iota(jnp.int32, (8, 128), 1)
    top = lax.broadcasted_iota(jnp.int32, (8, 128), 0) < 4
    even, left = (lane // 32) % 2 == 0, lane < 64

    def pack_rows(t, carry):
        for half in range(2):
            v = [
                acc[pl.ds(pl.multiple_of(t * 32 + i * 8, 8), 8), half * 128 : half * 128 + 128] for i in range(4)
            ]
            u = []
            for h in range(2):
                u.append(jnp.where(top, v[h], pltpu.roll(v[2 + h], 4, 0)))
                u.append(jnp.where(top, pltpu.roll(v[h], 4, 0), v[2 + h]))
            w = [[None, None], [None, None]]
            for a in range(2):
                w[a][0] = jnp.where(even, u[2 * a], pltpu.roll(u[2 * a + 1], 32, 1))
                w[a][1] = jnp.where(even, pltpu.roll(u[2 * a], 96, 1), u[2 * a + 1])
            for y0 in range(2):
                for b in range(2):
                    if b == 0:
                        tile = jnp.where(left, w[0][y0], pltpu.roll(w[1][y0], 64, 1))
                    else:
                        tile = jnp.where(left, pltpu.roll(w[0][y0], 64, 1), w[1][y0])
                    place = t * 8 + half * 4 + 2 * b + y0
                    pack[0, place] = tile[0:4]
                    pack[1, place] = tile[4:8]
        return carry

    lax.fori_loop(0, SAMP // 2, pack_rows, 0, unroll=True)

    me = samp * PAR + par

    x, z, core, y = samp // 4, ((samp // 2) % 2) * 2 + par // 4, samp % 2, par % 4
    xs, ys, zs = ([(v + d) % 4 for d in range(4)] for v in (x, y, z))
    for dx, dy, dz, dc in OTHERS:
        to_c = (core + dc) % 2
        chip_s, to_p = xs[dx] * 2 + zs[dz] // 2, (zs[dz] % 2) * 4 + ys[dy]
        pltpu.make_async_remote_copy(
            src_ref=pack.at[to_c, chip_s * PAR + to_p],
            dst_ref=parts.at[me],
            send_sem=r_send,
            recv_sem=r_recv,
            device_id=(chip_s * 2 + to_c, to_p),
            device_id_type=MESH,
        ).start()
    parts[me] = pack[samp % 2, (samp // 2) * PAR + par]

    got = parts.at[pl.ds(0, SAMP * PAR - 1)]
    pltpu.make_async_copy(got, got, r_recv).wait()
    tile = jnp.sum(parts[...], axis=0)
    row = samp * ROWS + lax.broadcasted_iota(jnp.int32, (4, 32), 0)
    col = par * 32 + lax.broadcasted_iota(jnp.int32, (4, 32), 1)
    for g in range(4):
        shift = jnp.where(row + 4 * g == col, diag_shift, 0.0)
        o_ref[4 * g : 4 * g + 4, :] = tile[:, 32 * g : 32 * g + 32] / TOTAL + shift

    pltpu.make_async_copy(got, got, r_send).wait()
    sent = full.at[pl.ds(0, TOTAL - ROWS), :]
    pltpu.make_async_copy(sent, sent, a_send).wait()


def body(log_derivs):
    share = log_derivs.shape[1] // SAMP
    return pl.pallas_call(
        kernel,
        out_shape=jax.ShapeDtypeStruct((ROWS, TOTAL // PAR), jnp.float32),
        in_specs=[pl.BlockSpec(memory_space=pl.ANY)],
        out_specs=pl.BlockSpec(memory_space=pltpu.VMEM),
        scratch_shapes=[
            pltpu.VMEM((TOTAL, share), jnp.float32),
            pltpu.VMEM((TOTAL, TOTAL), jnp.float32),
            pltpu.VMEM((2, SAMP * PAR // 2, 4, 128), jnp.float32),
            pltpu.VMEM((SAMP * PAR, 4, 128), jnp.float32),
            pltpu.SemaphoreType.DMA,
            pltpu.SemaphoreType.DMA,
            pltpu.SemaphoreType.DMA((CHUNKS,)),
            pltpu.SemaphoreType.DMA,
            pltpu.SemaphoreType.DMA,
        ],
        compiler_params=pltpu.CompilerParams(
            collective_id=0, has_side_effects=True, vmem_limit_bytes=60 * 1024 * 1024
        ),
        cost_estimate=pl.CostEstimate(flops=3 * 2 * TOTAL * TOTAL * share, bytes_accessed=2 << 20, transcendentals=0),
        name="sample_kernel",
    )(log_derivs)


def solution(mesh):
    return jax.shard_map(
        body,
        mesh=mesh,
        in_specs=(P("samp", "par"),),
        out_specs=P("samp", "par"),
        check_vma=False,
    )
```

```python
import functools

import jax
import jax.numpy as jnp
from jax import lax
from jax.experimental import pallas as pl
from jax.experimental.pallas import tpu as pltpu
from jax.sharding import PartitionSpec as P

diag_shift = 0.01
MESH = pl.DeviceIdType.MESH

ROWS = 16
SAMP = 16
PAR = 8
TOTAL = ROWS * SAMP
CHUNKS = 4

PARTNERS = [
    (2, 1, 0), (2, 1, 1), (1, 1, 0), (3, 1, 1), (1, 1, 1), (3, 1, 0), (2, 0, 0), (2, 0, 1),
    (0, 1, 0), (0, 1, 1), (1, 0, 0), (3, 0, 1), (1, 0, 1), (3, 0, 0), (0, 0, 1),
]


EARLY = [(0, 0, 0), (3, 0, 0), (1, 0, 0), (2, 0, 0)]


def is_later(x, y, z):
    return y + z > 0


def turns(value, size):
    return [value] + [jnp.where(value + d < size, value + d, value + d - size) for d in range(1, size)]


def ring_distance(delta):
    return min(delta, 4 - delta)


OTHERS = sorted(
    [(a, b, c, d) for a in range(4) for b in range(4) for c in range(4) for d in range(2) if a + b + c + d > 0],
    key=lambda k: -3 * sum(ring_distance(i) for i in k[:3]) - k[3],
)


def kernel(x_ref, o_ref, full, acc, pack, parts, local_sem, a_send, a_recv, r_send, r_recv):
    samp, par = lax.axis_index("samp"), lax.axis_index("par")
    share = full.shape[1]
    width = share // CHUNKS

    xs, highs, cores = turns(lax.div(samp, 4), 4), turns(lax.rem(lax.div(samp, 2), 2), 2), turns(lax.rem(samp, 2), 2)
    lows, ys = turns(lax.div(par, 4), 2), turns(lax.rem(par, 4), 4)
    partners = [xs[dx] * 4 + highs[dz] * 2 + cores[dc] for dx, dz, dc in PARTNERS]
    par_mates = [lows[dz] * 4 + ys[dy] for dz in range(2) for dy in range(4) if dz + dy > 0]

    barrier = pltpu.get_barrier_semaphore()
    for to in partners:
        pl.semaphore_signal(barrier, inc=1, device_id=(to, par), device_id_type=MESH)
    for to in par_mates:
        pl.semaphore_signal(barrier, inc=1, device_id=(samp, to), device_id_type=MESH)

    own = pl.ds(pl.multiple_of(samp * ROWS, ROWS), ROWS)
    keep = pltpu.make_async_copy(
        x_ref.at[:, pl.ds(pl.multiple_of(samp * share, share), share)], full.at[own, :], local_sem
    )
    keep.start()
    acc[...] = jnp.zeros_like(acc)
    pl.semaphore_wait(barrier, SAMP + PAR - 2)

    def send_chunk(k, carry):
        for to in partners:
            pltpu.make_async_remote_copy(
                src_ref=x_ref.at[:, pl.ds(pl.multiple_of(to * share + k * width, width), width)],
                dst_ref=full.at[own, pl.ds(pl.multiple_of(k * width, width), width)],
                send_sem=a_send,
                recv_sem=a_recv.at[k],
                device_id=(to, par),
                device_id_type=MESH,
            ).start()
        return carry

    lax.fori_loop(0, CHUNKS, send_chunk, 0)
    keep.wait()

    def gram_chunk(k, carry):
        cols = pl.ds(pl.multiple_of(k * width, width), width)
        got = full.at[pl.ds(0, TOTAL - ROWS), cols]
        pltpu.make_async_copy(got, got, a_recv.at[k]).wait()
        block = full[:, cols]
        block = block - jnp.sum(block, axis=0, keepdims=True) / TOTAL
        high = block.astype(jnp.bfloat16)
        low = (block - high.astype(jnp.float32)).astype(jnp.bfloat16)

        def dot(a, b):
            return lax.dot_general(a, b, (((1,), (1,)), ((), ())), preferred_element_type=jnp.float32)

        acc[...] += dot(high, high) + (dot(high, low) + dot(low, high))
        return carry

    lax.fori_loop(0, CHUNKS, gram_chunk, 0)

    lane = lax.broadcasted_iota(jnp.int32, (8, 128), 1)
    top = lax.broadcasted_iota(jnp.int32, (8, 128), 0) < 4
    even, left = (lane // 32) % 2 == 0, lane < 64

    def pack_rows(t, carry):
        for half in range(2):
            v = [
                acc[pl.ds(pl.multiple_of(t * 32 + i * 8, 8), 8), half * 128 : half * 128 + 128] for i in range(4)
            ]
            u = []
            for h in range(2):
                u.append(jnp.where(top, v[h], pltpu.roll(v[2 + h], 4, 0)))
                u.append(jnp.where(top, pltpu.roll(v[h], 4, 0), v[2 + h]))
            w = [[None, None], [None, None]]
            for a in range(2):
                w[a][0] = jnp.where(even, u[2 * a], pltpu.roll(u[2 * a + 1], 32, 1))
                w[a][1] = jnp.where(even, pltpu.roll(u[2 * a], 96, 1), u[2 * a + 1])
            for y0 in range(2):
                for b in range(2):
                    if b == 0:
                        tile = jnp.where(left, w[0][y0], pltpu.roll(w[1][y0], 64, 1))
                    else:
                        tile = jnp.where(left, pltpu.roll(w[0][y0], 64, 1), w[1][y0])
                    place = t * 8 + half * 4 + 2 * b + y0
                    pack[0, place] = tile[0:4]
                    pack[1, place] = tile[4:8]
        return carry

    lax.fori_loop(0, SAMP // 2, pack_rows, 0, unroll=True)

    me = samp * PAR + par

    zs = turns(highs[0] * 2 + lows[0], 4)
    zs_high = [lax.div(v, 2) for v in zs]
    zs_low = [v - 2 * h for v, h in zip(zs, zs_high)]

    def send_tile(dx, dy, dz, dc):
        chip_s, to_p = xs[dx] * 2 + zs_high[dz], zs_low[dz] * 4 + ys[dy]
        pltpu.make_async_remote_copy(
            src_ref=pack.at[cores[dc], chip_s * PAR + to_p],
            dst_ref=parts.at[me],
            send_sem=r_send,
            recv_sem=r_recv,
            device_id=(chip_s * 2 + cores[dc], to_p),
            device_id_type=MESH,
        ).start()

    def send_first(ax, ay, az):
        @pl.when((xs[0] != ax) | (ys[0] != ay) | (zs[0] != az))
        def _():
            chip_s, to_p = ax * 2 + az // 2, (az % 2) * 4 + ay
            for c in (1, 0):
                pltpu.make_async_remote_copy(
                    src_ref=pack.at[c, chip_s * PAR + to_p],
                    dst_ref=parts.at[me],
                    send_sem=r_send,
                    recv_sem=r_recv,
                    device_id=(chip_s * 2 + c, to_p),
                    device_id_type=MESH,
                ).start()

    for chip in EARLY:
        send_first(*chip)
    for dx, dy, dz, dc in OTHERS:
        if dx + dy + dz == 0:
            send_tile(dx, dy, dz, dc)
        else:
            pl.when(is_later(xs[dx], ys[dy], zs[dz]))(functools.partial(send_tile, dx, dy, dz, dc))
    parts[me] = pack[cores[0], (xs[0] * 2 + highs[0]) * PAR + par]

    got = parts.at[pl.ds(0, SAMP * PAR - 1)]
    pltpu.make_async_copy(got, got, r_recv).wait()
    tile = jnp.sum(parts[...], axis=0)
    row = samp * ROWS + lax.broadcasted_iota(jnp.int32, (4, 32), 0)
    col = par * 32 + lax.broadcasted_iota(jnp.int32, (4, 32), 1)
    for g in range(4):
        shift = jnp.where(row + 4 * g == col, diag_shift, 0.0)
        o_ref[4 * g : 4 * g + 4, :] = tile[:, 32 * g : 32 * g + 32] / TOTAL + shift

    pltpu.make_async_copy(got, got, r_send).wait()
    sent = full.at[pl.ds(0, TOTAL - ROWS), :]
    pltpu.make_async_copy(sent, sent, a_send).wait()


def body(log_derivs):
    share = log_derivs.shape[1] // SAMP
    return pl.pallas_call(
        kernel,
        out_shape=jax.ShapeDtypeStruct((ROWS, TOTAL // PAR), jnp.float32),
        in_specs=[pl.BlockSpec(memory_space=pl.ANY)],
        out_specs=pl.BlockSpec(memory_space=pltpu.VMEM),
        scratch_shapes=[
            pltpu.VMEM((TOTAL, share), jnp.float32),
            pltpu.VMEM((TOTAL, TOTAL), jnp.float32),
            pltpu.VMEM((2, SAMP * PAR // 2, 4, 128), jnp.float32),
            pltpu.VMEM((SAMP * PAR, 4, 128), jnp.float32),
            pltpu.SemaphoreType.DMA,
            pltpu.SemaphoreType.DMA,
            pltpu.SemaphoreType.DMA((CHUNKS,)),
            pltpu.SemaphoreType.DMA,
            pltpu.SemaphoreType.DMA,
        ],
        compiler_params=pltpu.CompilerParams(
            collective_id=0, has_side_effects=True, vmem_limit_bytes=60 * 1024 * 1024
        ),
        cost_estimate=pl.CostEstimate(flops=3 * 2 * TOTAL * TOTAL * share, bytes_accessed=2 << 20, transcendentals=0),
        name="sample_kernel",
    )(log_derivs)


def solution(mesh):
    return jax.shard_map(
        body,
        mesh=mesh,
        in_specs=(P("samp", "par"),),
        out_specs=P("samp", "par"),
        check_vma=False,
    )
```

```python
import functools

import jax
import jax.numpy as jnp
from jax import lax
from jax.experimental import pallas as pl
from jax.experimental.pallas import tpu as pltpu
from jax.sharding import PartitionSpec as P

diag_shift = 0.01
MESH = pl.DeviceIdType.MESH

ROWS = 16
SAMP = 16
PAR = 8
TOTAL = ROWS * SAMP
CHUNKS = 4

PARTNERS = [
    (2, 1, 0), (2, 1, 1), (1, 1, 0), (3, 1, 0), (1, 1, 1), (3, 1, 1), (2, 0, 0), (2, 0, 1),
    (0, 1, 0), (0, 1, 1), (1, 0, 0), (3, 0, 0), (1, 0, 1), (3, 0, 1), (0, 0, 1),
]


LEAD = (0, 0, 0)
EARLY = [(3, 0, 0), (1, 0, 0), (2, 0, 0), (0, 1, 0), (0, 0, 1)]


def is_later(x, y, z):
    return (y + z > 0) & (x + y + z != 1)


def turns(value, size):
    return [value] + [jnp.where(value + d < size, value + d, value + d - size) for d in range(1, size)]


def ring_distance(delta):
    return min(delta, 4 - delta)


OTHERS = sorted(
    [(a, b, c, d) for a in range(4) for b in range(4) for c in range(4) for d in range(2) if a + b + c + d > 0],
    key=lambda k: -3 * sum(ring_distance(i) for i in k[:3]) - k[3],
)


def kernel(x_ref, o_ref, full, acc, lead, pack, parts, local_sem, a_send, a_recv, r_send, r_recv):
    samp, par = lax.axis_index("samp"), lax.axis_index("par")
    share = full.shape[1]
    width = share // CHUNKS

    xs, highs, cores = turns(lax.div(samp, 4), 4), turns(lax.rem(lax.div(samp, 2), 2), 2), turns(lax.rem(samp, 2), 2)
    lows, ys = turns(lax.div(par, 4), 2), turns(lax.rem(par, 4), 4)
    partners = [xs[dx] * 4 + highs[dz] * 2 + cores[dc] for dx, dz, dc in PARTNERS]
    par_mates = [lows[dz] * 4 + ys[dy] for dz in range(2) for dy in range(4) if dz + dy > 0]

    barrier = pltpu.get_barrier_semaphore()
    for to in partners:
        pl.semaphore_signal(barrier, inc=1, device_id=(to, par), device_id_type=MESH)
    for to in par_mates:
        pl.semaphore_signal(barrier, inc=1, device_id=(samp, to), device_id_type=MESH)

    own = pl.ds(pl.multiple_of(samp * ROWS, ROWS), ROWS)
    keep = pltpu.make_async_copy(
        x_ref.at[:, pl.ds(pl.multiple_of(samp * share, share), share)], full.at[own, :], local_sem
    )
    keep.start()
    acc[...] = jnp.zeros_like(acc)
    pl.semaphore_wait(barrier, SAMP + PAR - 2)

    def send_chunk(k, carry):
        for to in partners:
            pltpu.make_async_remote_copy(
                src_ref=x_ref.at[:, pl.ds(pl.multiple_of(to * share + k * width, width), width)],
                dst_ref=full.at[own, pl.ds(pl.multiple_of(k * width, width), width)],
                send_sem=a_send,
                recv_sem=a_recv.at[k],
                device_id=(to, par),
                device_id_type=MESH,
            ).start()
        return carry

    lax.fori_loop(0, CHUNKS, send_chunk, 0)
    keep.wait()

    def dot(a, b):
        return lax.dot_general(a, b, (((1,), (1,)), ((), ())), preferred_element_type=jnp.float32)

    def halves(k):
        cols = pl.ds(pl.multiple_of(k * width, width), width)
        got = full.at[pl.ds(0, TOTAL - ROWS), cols]
        pltpu.make_async_copy(got, got, a_recv.at[k]).wait()
        block = full[:, cols]
        block = block - jnp.sum(block, axis=0, keepdims=True) / TOTAL
        high = block.astype(jnp.bfloat16)
        return high, (block - high.astype(jnp.float32)).astype(jnp.bfloat16)

    def gram_of(high, low, rows=TOTAL, cols=TOTAL):
        return dot(high[:rows], high[:cols]) + (dot(high[:rows], low[:cols]) + dot(low[:rows], high[:cols]))

    def gram_chunk(k, carry):
        acc[...] += gram_of(*halves(k))
        return carry

    lane = lax.broadcasted_iota(jnp.int32, (8, 128), 1)
    top = lax.broadcasted_iota(jnp.int32, (8, 128), 0) < 4
    even, left = (lane // 32) % 2 == 0, lane < 64

    def packed(v):
        u = []
        for h in range(2):
            u.append(jnp.where(top, v[h], pltpu.roll(v[2 + h], 4, 0)))
            u.append(jnp.where(top, pltpu.roll(v[h], 4, 0), v[2 + h]))
        w = [[None, None], [None, None]]
        for a in range(2):
            w[a][0] = jnp.where(even, u[2 * a], pltpu.roll(u[2 * a + 1], 32, 1))
            w[a][1] = jnp.where(even, pltpu.roll(u[2 * a], 96, 1), u[2 * a + 1])
        tiles = []
        for b in range(2):
            for y0 in range(2):
                if b == 0:
                    tiles.append(jnp.where(left, w[0][y0], pltpu.roll(w[1][y0], 64, 1)))
                else:
                    tiles.append(jnp.where(left, pltpu.roll(w[0][y0], 64, 1), w[1][y0]))
        return tiles

    lax.fori_loop(0, CHUNKS - 1, gram_chunk, 0)
    high, low = halves(CHUNKS - 1)

    me = samp * PAR + par
    zs = turns(highs[0] * 2 + lows[0], 4)
    zs_high = [lax.div(v, 2) for v in zs]
    zs_low = [v - 2 * h for v, h in zip(zs, zs_high)]

    def send_to(src, chip_s, to_p, c):
        pltpu.make_async_remote_copy(
            src_ref=src,
            dst_ref=parts.at[me],
            send_sem=r_send,
            recv_sem=r_recv,
            device_id=(chip_s * 2 + c, to_p),
            device_id_type=MESH,
        ).start()

    def elsewhere(chip):
        return (xs[0] != chip[0]) | (ys[0] != chip[1]) | (zs[0] != chip[2])

    block = acc[0:32, 0:128] + gram_of(high, low, 32, 128)
    tile = packed([block[8 * i : 8 * i + 8] for i in range(4)])[0]
    lead[0] = tile[0:4]
    lead[1] = tile[4:8]

    @pl.when(elsewhere(LEAD))
    def _():
        for c in (1, 0):
            send_to(lead.at[c], 0, 0, c)

    acc[...] += gram_of(high, low)

    def pack_rows(t, carry):
        for half in range(2):
            v = [
                acc[pl.ds(pl.multiple_of(t * 32 + i * 8, 8), 8), half * 128 : half * 128 + 128] for i in range(4)
            ]
            for y, tile in enumerate(packed(v)):
                pack[0, t * 8 + half * 4 + y] = tile[0:4]
                pack[1, t * 8 + half * 4 + y] = tile[4:8]
        return carry

    lax.fori_loop(0, SAMP // 2, pack_rows, 0, unroll=True)

    for x, y, z in EARLY:
        @pl.when(elsewhere((x, y, z)))
        def _():
            chip_s, to_p = x * 2 + z // 2, (z % 2) * 4 + y
            for c in (1, 0):
                send_to(pack.at[c, chip_s * PAR + to_p], chip_s, to_p, c)

    def send_other(dx, dy, dz, dc):
        chip_s, to_p = xs[dx] * 2 + zs_high[dz], zs_low[dz] * 4 + ys[dy]
        send_to(pack.at[cores[dc], chip_s * PAR + to_p], chip_s, to_p, cores[dc])

    for dx, dy, dz, dc in OTHERS:
        if dx + dy + dz == 0:
            send_other(dx, dy, dz, dc)
        else:
            pl.when(is_later(xs[dx], ys[dy], zs[dz]))(functools.partial(send_other, dx, dy, dz, dc))

    parts[me] = pack[cores[0], (xs[0] * 2 + highs[0]) * PAR + par]

    got = parts.at[pl.ds(0, SAMP * PAR - 1)]
    pltpu.make_async_copy(got, got, r_recv).wait()
    tile = jnp.sum(parts[...], axis=0)
    row = samp * ROWS + lax.broadcasted_iota(jnp.int32, (4, 32), 0)
    col = par * 32 + lax.broadcasted_iota(jnp.int32, (4, 32), 1)
    for g in range(4):
        shift = jnp.where(row + 4 * g == col, diag_shift, 0.0)
        o_ref[4 * g : 4 * g + 4, :] = tile[:, 32 * g : 32 * g + 32] / TOTAL + shift

    pltpu.make_async_copy(got, got, r_send).wait()
    sent = full.at[pl.ds(0, TOTAL - ROWS), :]
    pltpu.make_async_copy(sent, sent, a_send).wait()


def body(log_derivs):
    share = log_derivs.shape[1] // SAMP
    return pl.pallas_call(
        kernel,
        out_shape=jax.ShapeDtypeStruct((ROWS, TOTAL // PAR), jnp.float32),
        in_specs=[pl.BlockSpec(memory_space=pl.ANY)],
        out_specs=pl.BlockSpec(memory_space=pltpu.VMEM),
        scratch_shapes=[
            pltpu.VMEM((TOTAL, share), jnp.float32),
            pltpu.VMEM((TOTAL, TOTAL), jnp.float32),
            pltpu.VMEM((2, 4, 128), jnp.float32),
            pltpu.VMEM((2, SAMP * PAR // 2, 4, 128), jnp.float32),
            pltpu.VMEM((SAMP * PAR, 4, 128), jnp.float32),
            pltpu.SemaphoreType.DMA,
            pltpu.SemaphoreType.DMA,
            pltpu.SemaphoreType.DMA((CHUNKS,)),
            pltpu.SemaphoreType.DMA,
            pltpu.SemaphoreType.DMA,
        ],
        compiler_params=pltpu.CompilerParams(
            collective_id=0, has_side_effects=True, vmem_limit_bytes=60 * 1024 * 1024
        ),
        cost_estimate=pl.CostEstimate(flops=3 * 2 * TOTAL * TOTAL * share, bytes_accessed=2 << 20, transcendentals=0),
        name="sample_kernel",
    )(log_derivs)


def solution(mesh):
    return jax.shard_map(
        body,
        mesh=mesh,
        in_specs=(P("samp", "par"),),
        out_specs=P("samp", "par"),
        check_vma=False,
    )
```

```python
import functools

import jax
import jax.numpy as jnp
from jax import lax
from jax.experimental import pallas as pl
from jax.experimental.pallas import tpu as pltpu
from jax.sharding import PartitionSpec as P

diag_shift = 0.01
MESH = pl.DeviceIdType.MESH

ROWS = 16
SAMP = 16
PAR = 8
TOTAL = ROWS * SAMP
CHUNKS = 4

PARTNERS = [
    (2, 1, 0), (2, 1, 1), (1, 1, 0), (3, 1, 0), (1, 1, 1), (3, 1, 1), (2, 0, 0), (2, 0, 1),
    (0, 1, 0), (0, 1, 1), (1, 0, 0), (3, 0, 0), (1, 0, 1), (3, 0, 1), (0, 0, 1),
]


LEAD = (0, 0, 0)
EARLY = [(3, 0, 0), (1, 0, 0), (2, 0, 0), (0, 1, 0), (0, 0, 1)]


def is_later(x, y, z):
    return (y + z > 0) & (x + y + z != 1)


def turns(value, size):
    return [value] + [jnp.where(value + d < size, value + d, value + d - size) for d in range(1, size)]


def ring_distance(delta):
    return min(delta, 4 - delta)


OTHERS = sorted(
    [(a, b, c, d) for a in range(4) for b in range(4) for c in range(4) for d in range(2) if a + b + c + d > 0],
    key=lambda k: -3 * sum(ring_distance(i) for i in k[:3]) - k[3],
)


def kernel(x_ref, o_ref, full, acc, lead, pack, parts, local_sem, a_send, a_recv, r_send, r_recv):
    samp, par = lax.axis_index("samp"), lax.axis_index("par")
    share = full.shape[1]
    width = share // CHUNKS

    xs, highs, cores = turns(lax.div(samp, 4), 4), turns(lax.rem(lax.div(samp, 2), 2), 2), turns(lax.rem(samp, 2), 2)
    lows, ys = turns(lax.div(par, 4), 2), turns(lax.rem(par, 4), 4)
    partners = [xs[dx] * 4 + highs[dz] * 2 + cores[dc] for dx, dz, dc in PARTNERS]
    par_mates = [lows[dz] * 4 + ys[dy] for dz in range(2) for dy in range(4) if dz + dy > 0]

    barrier = pltpu.get_barrier_semaphore()
    for to in partners:
        pl.semaphore_signal(barrier, inc=1, device_id=(to, par), device_id_type=MESH)
    for to in par_mates:
        pl.semaphore_signal(barrier, inc=1, device_id=(samp, to), device_id_type=MESH)

    own = pl.ds(pl.multiple_of(samp * ROWS, ROWS), ROWS)
    keep = pltpu.make_async_copy(
        x_ref.at[:, pl.ds(pl.multiple_of(samp * share, share), share)], full.at[own, :], local_sem
    )
    keep.start()
    acc[...] = jnp.zeros_like(acc)
    pl.semaphore_wait(barrier, SAMP + PAR - 2)

    def send_chunk(k, carry):
        for to in partners:
            pltpu.make_async_remote_copy(
                src_ref=x_ref.at[:, pl.ds(pl.multiple_of(to * share + k * width, width), width)],
                dst_ref=full.at[own, pl.ds(pl.multiple_of(k * width, width), width)],
                send_sem=a_send,
                recv_sem=a_recv.at[k],
                device_id=(to, par),
                device_id_type=MESH,
            ).start()
        return carry

    lax.fori_loop(0, CHUNKS, send_chunk, 0)
    keep.wait()

    def dot(a, b):
        return lax.dot_general(a, b, (((1,), (1,)), ((), ())), preferred_element_type=jnp.float32)

    def arrived(k):
        cols = pl.ds(pl.multiple_of(k * width, width), width)
        got = full.at[pl.ds(0, TOTAL - ROWS), cols]
        pltpu.make_async_copy(got, got, a_recv.at[k]).wait()
        return cols, jnp.sum(full[:, cols], axis=0, keepdims=True) / TOTAL

    def halves(cols, mean, rows=TOTAL):
        block = full[:rows, cols] - mean
        high = block.astype(jnp.bfloat16)
        return high, (block - high.astype(jnp.float32)).astype(jnp.bfloat16)

    def gram_of(high, low):
        return dot(high, high) + (dot(high, low) + dot(low, high))

    def gram_chunk(k, carry):
        acc[...] += gram_of(*halves(*arrived(k)))
        return carry

    lane = lax.broadcasted_iota(jnp.int32, (8, 128), 1)
    top = lax.broadcasted_iota(jnp.int32, (8, 128), 0) < 4
    even, left = (lane // 32) % 2 == 0, lane < 64

    def packed(v):
        u = []
        for h in range(2):
            u.append(jnp.where(top, v[h], pltpu.roll(v[2 + h], 4, 0)))
            u.append(jnp.where(top, pltpu.roll(v[h], 4, 0), v[2 + h]))
        w = [[None, None], [None, None]]
        for a in range(2):
            w[a][0] = jnp.where(even, u[2 * a], pltpu.roll(u[2 * a + 1], 32, 1))
            w[a][1] = jnp.where(even, pltpu.roll(u[2 * a], 96, 1), u[2 * a + 1])
        tiles = []
        for b in range(2):
            for y0 in range(2):
                if b == 0:
                    tiles.append(jnp.where(left, w[0][y0], pltpu.roll(w[1][y0], 64, 1)))
                else:
                    tiles.append(jnp.where(left, pltpu.roll(w[0][y0], 64, 1), w[1][y0]))
        return tiles

    lax.fori_loop(0, CHUNKS - 1, gram_chunk, 0)
    cols, mean = arrived(CHUNKS - 1)

    me = samp * PAR + par
    zs = turns(highs[0] * 2 + lows[0], 4)
    zs_high = [lax.div(v, 2) for v in zs]
    zs_low = [v - 2 * h for v, h in zip(zs, zs_high)]

    def send_to(src, chip_s, to_p, c):
        pltpu.make_async_remote_copy(
            src_ref=src,
            dst_ref=parts.at[me],
            send_sem=r_send,
            recv_sem=r_recv,
            device_id=(chip_s * 2 + c, to_p),
            device_id_type=MESH,
        ).start()

    def elsewhere(chip):
        return (xs[0] != chip[0]) | (ys[0] != chip[1]) | (zs[0] != chip[2])

    corner = acc[0:32, 0:32] + gram_of(*halves(cols, mean, 32))
    corner = jnp.concatenate([corner, jnp.zeros((32, 96), jnp.float32)], axis=1)
    tile = packed([corner[8 * i : 8 * i + 8] for i in range(4)])[0]
    lead[0] = tile[0:4]
    lead[1] = tile[4:8]

    @pl.when(elsewhere(LEAD))
    def _():
        for c in (1, 0):
            send_to(lead.at[c], 0, 0, c)

    acc[...] += gram_of(*halves(cols, mean))

    def pack_rows(t, carry):
        for half in range(2):
            v = [
                acc[pl.ds(pl.multiple_of(t * 32 + i * 8, 8), 8), half * 128 : half * 128 + 128] for i in range(4)
            ]
            for y, tile in enumerate(packed(v)):
                pack[0, t * 8 + half * 4 + y] = tile[0:4]
                pack[1, t * 8 + half * 4 + y] = tile[4:8]
        return carry

    lax.fori_loop(0, SAMP // 2, pack_rows, 0, unroll=True)

    for x, y, z in EARLY:
        @pl.when(elsewhere((x, y, z)))
        def _():
            chip_s, to_p = x * 2 + z // 2, (z % 2) * 4 + y
            for c in (1, 0):
                send_to(pack.at[c, chip_s * PAR + to_p], chip_s, to_p, c)

    def send_other(dx, dy, dz, dc):
        chip_s, to_p = xs[dx] * 2 + zs_high[dz], zs_low[dz] * 4 + ys[dy]
        send_to(pack.at[cores[dc], chip_s * PAR + to_p], chip_s, to_p, cores[dc])

    for dx, dy, dz, dc in OTHERS:
        if dx + dy + dz == 0:
            send_other(dx, dy, dz, dc)
        else:
            pl.when(is_later(xs[dx], ys[dy], zs[dz]))(functools.partial(send_other, dx, dy, dz, dc))

    parts[me] = pack[cores[0], (xs[0] * 2 + highs[0]) * PAR + par]

    got = parts.at[pl.ds(0, SAMP * PAR - 1)]
    pltpu.make_async_copy(got, got, r_recv).wait()
    total = parts[...]
    while total.shape[0] > 1:
        half = total.shape[0] // 2
        total = total[:half] + total[half:]
    tile = total[0]
    row = samp * ROWS + lax.broadcasted_iota(jnp.int32, (4, 32), 0)
    col = par * 32 + lax.broadcasted_iota(jnp.int32, (4, 32), 1)
    for g in range(4):
        shift = jnp.where(row + 4 * g == col, diag_shift, 0.0)
        o_ref[4 * g : 4 * g + 4, :] = tile[:, 32 * g : 32 * g + 32] / TOTAL + shift

    pltpu.make_async_copy(got, got, r_send).wait()
    sent = full.at[pl.ds(0, TOTAL - ROWS), :]
    pltpu.make_async_copy(sent, sent, a_send).wait()


def body(log_derivs):
    share = log_derivs.shape[1] // SAMP
    return pl.pallas_call(
        kernel,
        out_shape=jax.ShapeDtypeStruct((ROWS, TOTAL // PAR), jnp.float32),
        in_specs=[pl.BlockSpec(memory_space=pl.ANY)],
        out_specs=pl.BlockSpec(memory_space=pltpu.VMEM),
        scratch_shapes=[
            pltpu.VMEM((TOTAL, share), jnp.float32),
            pltpu.VMEM((TOTAL, TOTAL), jnp.float32),
            pltpu.VMEM((2, 4, 128), jnp.float32),
            pltpu.VMEM((2, SAMP * PAR // 2, 4, 128), jnp.float32),
            pltpu.VMEM((SAMP * PAR, 4, 128), jnp.float32),
            pltpu.SemaphoreType.DMA,
            pltpu.SemaphoreType.DMA,
            pltpu.SemaphoreType.DMA((CHUNKS,)),
            pltpu.SemaphoreType.DMA,
            pltpu.SemaphoreType.DMA,
        ],
        compiler_params=pltpu.CompilerParams(
            collective_id=0, has_side_effects=True, vmem_limit_bytes=60 * 1024 * 1024
        ),
        cost_estimate=pl.CostEstimate(flops=3 * 2 * TOTAL * TOTAL * share, bytes_accessed=2 << 20, transcendentals=0),
        name="sample_kernel",
    )(log_derivs)


def solution(mesh):
    return jax.shard_map(
        body,
        mesh=mesh,
        in_specs=(P("samp", "par"),),
        out_specs=P("samp", "par"),
        check_vma=False,
    )
```

```python
import functools

import jax
import jax.numpy as jnp
from jax import lax
from jax.experimental import pallas as pl
from jax.experimental.pallas import tpu as pltpu
from jax.sharding import PartitionSpec as P

diag_shift = 0.01
MESH = pl.DeviceIdType.MESH

ROWS = 16
SAMP = 16
PAR = 8
TOTAL = ROWS * SAMP
CHUNKS = 4

PARTNERS = [
    (2, 1, 0), (2, 1, 1), (1, 1, 0), (3, 1, 0), (1, 1, 1), (3, 1, 1), (2, 0, 0), (2, 0, 1),
    (0, 1, 0), (0, 1, 1), (1, 0, 0), (3, 0, 0), (1, 0, 1), (3, 0, 1), (0, 0, 1),
]


LEAD = (0, 0, 0)
EARLY = [(3, 0, 0), (1, 0, 0), (2, 0, 0), (0, 1, 0), (0, 0, 1)]


def is_later(x, y, z):
    return (y + z > 0) & (x + y + z != 1)


def turns(value, size):
    return [value] + [jnp.where(value + d < size, value + d, value + d - size) for d in range(1, size)]


def ring_distance(delta):
    return min(delta, 4 - delta)


OTHERS = sorted(
    [(a, b, c, d) for a in range(4) for b in range(4) for c in range(4) for d in range(2) if a + b + c + d > 0],
    key=lambda k: -3 * sum(ring_distance(i) for i in k[:3]) - k[3],
)


def kernel(x_ref, o_ref, full, acc, lead, pack, parts, held, stage_sem, local_sem, a_send, a_recv, r_send, r_recv):
    samp, par = lax.axis_index("samp"), lax.axis_index("par")
    share = full.shape[1]
    width = share // CHUNKS

    xs, highs, cores = turns(lax.div(samp, 4), 4), turns(lax.rem(lax.div(samp, 2), 2), 2), turns(lax.rem(samp, 2), 2)
    lows, ys = turns(lax.div(par, 4), 2), turns(lax.rem(par, 4), 4)
    partners = [xs[dx] * 4 + highs[dz] * 2 + cores[dc] for dx, dz, dc in PARTNERS]
    par_mates = [lows[dz] * 4 + ys[dy] for dz in range(2) for dy in range(4) if dz + dy > 0]

    stages = [
        pltpu.make_async_copy(x_ref.at[rows, :], held.at[rows, :], stage_sem.at[i])
        for i, rows in enumerate((pl.ds(0, 8), pl.ds(8, 8)))
    ]
    for stage in stages:
        stage.start()
    barrier = pltpu.get_barrier_semaphore()
    for to in partners:
        pl.semaphore_signal(barrier, inc=1, device_id=(to, par), device_id_type=MESH)
    for to in par_mates:
        pl.semaphore_signal(barrier, inc=1, device_id=(samp, to), device_id_type=MESH)

    own = pl.ds(pl.multiple_of(samp * ROWS, ROWS), ROWS)
    keep = pltpu.make_async_copy(
        x_ref.at[:, pl.ds(pl.multiple_of(samp * share, share), share)], full.at[own, :], local_sem
    )
    keep.start()
    acc[...] = jnp.zeros_like(acc)
    pl.semaphore_wait(barrier, SAMP + PAR - 2)

    def send_chunk(src, k):
        for to in partners:
            pltpu.make_async_remote_copy(
                src_ref=src.at[:, pl.ds(pl.multiple_of(to * share + k * width, width), width)],
                dst_ref=full.at[own, pl.ds(pl.multiple_of(k * width, width), width)],
                send_sem=a_send,
                recv_sem=a_recv.at[k],
                device_id=(to, par),
                device_id_type=MESH,
            ).start()

    send_chunk(x_ref, 0)
    for stage in stages:
        stage.wait()
    @pl.loop(1, CHUNKS)
    def _(k):
        send_chunk(held, k)

    keep.wait()

    def dot(a, b):
        return lax.dot_general(a, b, (((1,), (1,)), ((), ())), preferred_element_type=jnp.float32)

    def arrived(k):
        cols = pl.ds(pl.multiple_of(k * width, width), width)
        got = full.at[pl.ds(0, TOTAL - ROWS), cols]
        pltpu.make_async_copy(got, got, a_recv.at[k]).wait()
        return cols, jnp.sum(full[:, cols], axis=0, keepdims=True) / TOTAL

    def halves(cols, mean, rows=TOTAL):
        block = full[:rows, cols] - mean
        high = block.astype(jnp.bfloat16)
        return high, (block - high.astype(jnp.float32)).astype(jnp.bfloat16)

    def gram_of(high, low):
        return dot(high, high) + (dot(high, low) + dot(low, high))

    def gram_chunk(k, carry):
        acc[...] += gram_of(*halves(*arrived(k)))
        return carry

    lane = lax.broadcasted_iota(jnp.int32, (8, 128), 1)
    top = lax.broadcasted_iota(jnp.int32, (8, 128), 0) < 4
    even, left = (lane // 32) % 2 == 0, lane < 64

    def packed(v):
        u = []
        for h in range(2):
            u.append(jnp.where(top, v[h], pltpu.roll(v[2 + h], 4, 0)))
            u.append(jnp.where(top, pltpu.roll(v[h], 4, 0), v[2 + h]))
        w = [[None, None], [None, None]]
        for a in range(2):
            w[a][0] = jnp.where(even, u[2 * a], pltpu.roll(u[2 * a + 1], 32, 1))
            w[a][1] = jnp.where(even, pltpu.roll(u[2 * a], 96, 1), u[2 * a + 1])
        tiles = []
        for b in range(2):
            for y0 in range(2):
                if b == 0:
                    tiles.append(jnp.where(left, w[0][y0], pltpu.roll(w[1][y0], 64, 1)))
                else:
                    tiles.append(jnp.where(left, pltpu.roll(w[0][y0], 64, 1), w[1][y0]))
        return tiles

    lax.fori_loop(0, CHUNKS - 1, gram_chunk, 0)
    cols, mean = arrived(CHUNKS - 1)

    me = samp * PAR + par
    zs = turns(highs[0] * 2 + lows[0], 4)
    zs_high = [lax.div(v, 2) for v in zs]
    zs_low = [v - 2 * h for v, h in zip(zs, zs_high)]

    def send_to(src, chip_s, to_p, c):
        pltpu.make_async_remote_copy(
            src_ref=src,
            dst_ref=parts.at[me],
            send_sem=r_send,
            recv_sem=r_recv,
            device_id=(chip_s * 2 + c, to_p),
            device_id_type=MESH,
        ).start()

    def elsewhere(chip):
        return (xs[0] != chip[0]) | (ys[0] != chip[1]) | (zs[0] != chip[2])

    corner = acc[0:32, 0:32] + gram_of(*halves(cols, mean, 32))
    corner = jnp.concatenate([corner, jnp.zeros((32, 96), jnp.float32)], axis=1)
    tile = packed([corner[8 * i : 8 * i + 8] for i in range(4)])[0]
    lead[0] = tile[0:4]
    lead[1] = tile[4:8]

    @pl.when(elsewhere(LEAD))
    def _():
        for c in (1, 0):
            send_to(lead.at[c], 0, 0, c)

    acc[...] += gram_of(*halves(cols, mean))

    def pack_rows(t, carry):
        for half in range(2):
            v = [
                acc[pl.ds(pl.multiple_of(t * 32 + i * 8, 8), 8), half * 128 : half * 128 + 128] for i in range(4)
            ]
            for y, tile in enumerate(packed(v)):
                pack[0, t * 8 + half * 4 + y] = tile[0:4]
                pack[1, t * 8 + half * 4 + y] = tile[4:8]
        return carry

    lax.fori_loop(0, SAMP // 2, pack_rows, 0, unroll=True)

    for x, y, z in EARLY:
        @pl.when(elsewhere((x, y, z)))
        def _():
            chip_s, to_p = x * 2 + z // 2, (z % 2) * 4 + y
            for c in (1, 0):
                send_to(pack.at[c, chip_s * PAR + to_p], chip_s, to_p, c)

    def send_other(dx, dy, dz, dc):
        chip_s, to_p = xs[dx] * 2 + zs_high[dz], zs_low[dz] * 4 + ys[dy]
        send_to(pack.at[cores[dc], chip_s * PAR + to_p], chip_s, to_p, cores[dc])

    for dx, dy, dz, dc in OTHERS:
        if dx + dy + dz == 0:
            send_other(dx, dy, dz, dc)
        else:
            pl.when(is_later(xs[dx], ys[dy], zs[dz]))(functools.partial(send_other, dx, dy, dz, dc))

    parts[me] = pack[cores[0], (xs[0] * 2 + highs[0]) * PAR + par]

    got = parts.at[pl.ds(0, SAMP * PAR - 1)]
    pltpu.make_async_copy(got, got, r_recv).wait()
    total = parts[...]
    while total.shape[0] > 1:
        half = total.shape[0] // 2
        total = total[:half] + total[half:]
    tile = total[0]
    row = samp * ROWS + lax.broadcasted_iota(jnp.int32, (4, 32), 0)
    col = par * 32 + lax.broadcasted_iota(jnp.int32, (4, 32), 1)
    for g in range(4):
        shift = jnp.where(row + 4 * g == col, diag_shift, 0.0)
        o_ref[4 * g : 4 * g + 4, :] = tile[:, 32 * g : 32 * g + 32] / TOTAL + shift

    pltpu.make_async_copy(got, got, r_send).wait()
    sent = full.at[pl.ds(0, TOTAL - ROWS), :]
    pltpu.make_async_copy(sent, sent, a_send).wait()


def body(log_derivs):
    share = log_derivs.shape[1] // SAMP
    return pl.pallas_call(
        kernel,
        out_shape=jax.ShapeDtypeStruct((ROWS, TOTAL // PAR), jnp.float32),
        in_specs=[pl.BlockSpec(memory_space=pl.ANY)],
        out_specs=pl.BlockSpec(memory_space=pltpu.VMEM),
        scratch_shapes=[
            pltpu.VMEM((TOTAL, share), jnp.float32),
            pltpu.VMEM((TOTAL, TOTAL), jnp.float32),
            pltpu.VMEM((2, 4, 128), jnp.float32),
            pltpu.VMEM((2, SAMP * PAR // 2, 4, 128), jnp.float32),
            pltpu.VMEM((SAMP * PAR, 4, 128), jnp.float32),
            pltpu.VMEM(log_derivs.shape, jnp.float32),
            pltpu.SemaphoreType.DMA((2,)),
            pltpu.SemaphoreType.DMA,
            pltpu.SemaphoreType.DMA,
            pltpu.SemaphoreType.DMA((CHUNKS,)),
            pltpu.SemaphoreType.DMA,
            pltpu.SemaphoreType.DMA,
        ],
        compiler_params=pltpu.CompilerParams(
            collective_id=0, has_side_effects=True, vmem_limit_bytes=60 * 1024 * 1024
        ),
        cost_estimate=pl.CostEstimate(flops=3 * 2 * TOTAL * TOTAL * share, bytes_accessed=2 << 20, transcendentals=0),
        name="sample_kernel",
    )(log_derivs)


def solution(mesh):
    return jax.shard_map(
        body,
        mesh=mesh,
        in_specs=(P("samp", "par"),),
        out_specs=P("samp", "par"),
        check_vma=False,
    )
```

```python
import functools

import jax
import jax.numpy as jnp
from jax import lax
from jax.experimental import pallas as pl
from jax.experimental.pallas import tpu as pltpu
from jax.sharding import PartitionSpec as P

diag_shift = 0.01
MESH = pl.DeviceIdType.MESH

ROWS = 16
SAMP = 16
PAR = 8
TOTAL = ROWS * SAMP
CHUNKS = 4

PARTNERS = [
    (2, 1, 0), (2, 1, 1), (1, 1, 0), (3, 1, 0), (1, 1, 1), (3, 1, 1), (2, 0, 0), (2, 0, 1),
    (0, 1, 0), (0, 1, 1), (1, 0, 0), (3, 0, 0), (1, 0, 1), (3, 0, 1), (0, 0, 1),
]


LEAD = (0, 0, 0)
EARLY = [(3, 0, 0), (1, 0, 0), (2, 0, 0), (0, 1, 0), (0, 0, 1)]


def is_later(x, y, z):
    return (y + z > 0) & (x + y + z != 1)


def turns(value, size):
    return [value] + [jnp.where(value + d < size, value + d, value + d - size) for d in range(1, size)]


def ring_distance(delta):
    return min(delta, 4 - delta)


OTHERS = sorted(
    [(a, b, c, d) for a in range(4) for b in range(4) for c in range(4) for d in range(2) if a + b + c + d > 0],
    key=lambda k: -3 * sum(ring_distance(i) for i in k[:3]) - k[3],
)


def kernel(x_ref, o_ref, full, acc, lead, pack, parts, local_sem, a_send, a_recv, r_send, r_recv):
    samp, par = lax.axis_index("samp"), lax.axis_index("par")
    share = full.shape[1]
    width = share // CHUNKS

    xs, highs, cores = turns(lax.div(samp, 4), 4), turns(lax.rem(lax.div(samp, 2), 2), 2), turns(lax.rem(samp, 2), 2)
    lows, ys = turns(lax.div(par, 4), 2), turns(lax.rem(par, 4), 4)
    partners = [xs[dx] * 4 + highs[dz] * 2 + cores[dc] for dx, dz, dc in PARTNERS]
    par_mates = [lows[dz] * 4 + ys[dy] for dz in range(2) for dy in range(4) if dz + dy > 0]

    barrier = pltpu.get_barrier_semaphore()
    for to in partners:
        pl.semaphore_signal(barrier, inc=1, device_id=(to, par), device_id_type=MESH)
    for to in par_mates:
        pl.semaphore_signal(barrier, inc=1, device_id=(samp, to), device_id_type=MESH)

    own = pl.ds(pl.multiple_of(samp * ROWS, ROWS), ROWS)
    keep = pltpu.make_async_copy(
        x_ref.at[:, pl.ds(pl.multiple_of(samp * share, share), share)], full.at[own, :], local_sem
    )
    keep.start()
    acc[...] = jnp.zeros_like(acc)
    pl.semaphore_wait(barrier, SAMP + PAR - 2)

    for k in range(CHUNKS):
        turn = 8 * (CHUNKS - 1 - k) % len(partners)
        for to in partners[turn:] + partners[:turn]:
            pltpu.make_async_remote_copy(
                src_ref=x_ref.at[:, pl.ds(pl.multiple_of(to * share + k * width, width), width)],
                dst_ref=full.at[own, pl.ds(k * width, width)],
                send_sem=a_send,
                recv_sem=a_recv.at[k],
                device_id=(to, par),
                device_id_type=MESH,
            ).start()

    keep.wait()

    def dot(a, b):
        return lax.dot_general(a, b, (((1,), (1,)), ((), ())), preferred_element_type=jnp.float32)

    def arrived(k):
        cols = pl.ds(pl.multiple_of(k * width, width), width)
        got = full.at[pl.ds(0, TOTAL - ROWS), cols]
        pltpu.make_async_copy(got, got, a_recv.at[k]).wait()
        return cols, jnp.sum(full[:, cols], axis=0, keepdims=True) / TOTAL

    def halves(cols, mean, rows=TOTAL):
        block = full[:rows, cols] - mean
        high = block.astype(jnp.bfloat16)
        return high, (block - high.astype(jnp.float32)).astype(jnp.bfloat16)

    def gram_of(high, low):
        return dot(high, high) + (dot(high, low) + dot(low, high))

    def gram_chunk(k, carry):
        acc[...] += gram_of(*halves(*arrived(k)))
        return carry

    lane = lax.broadcasted_iota(jnp.int32, (8, 128), 1)
    top = lax.broadcasted_iota(jnp.int32, (8, 128), 0) < 4
    even, left = (lane // 32) % 2 == 0, lane < 64

    def packed(v):
        u = []
        for h in range(2):
            u.append(jnp.where(top, v[h], pltpu.roll(v[2 + h], 4, 0)))
            u.append(jnp.where(top, pltpu.roll(v[h], 4, 0), v[2 + h]))
        w = [[None, None], [None, None]]
        for a in range(2):
            w[a][0] = jnp.where(even, u[2 * a], pltpu.roll(u[2 * a + 1], 32, 1))
            w[a][1] = jnp.where(even, pltpu.roll(u[2 * a], 96, 1), u[2 * a + 1])
        tiles = []
        for b in range(2):
            for y0 in range(2):
                if b == 0:
                    tiles.append(jnp.where(left, w[0][y0], pltpu.roll(w[1][y0], 64, 1)))
                else:
                    tiles.append(jnp.where(left, pltpu.roll(w[0][y0], 64, 1), w[1][y0]))
        return tiles

    lax.fori_loop(0, CHUNKS - 1, gram_chunk, 0)
    cols, mean = arrived(CHUNKS - 1)

    me = samp * PAR + par
    zs = turns(highs[0] * 2 + lows[0], 4)
    zs_high = [lax.div(v, 2) for v in zs]
    zs_low = [v - 2 * h for v, h in zip(zs, zs_high)]

    def send_to(src, chip_s, to_p, c):
        pltpu.make_async_remote_copy(
            src_ref=src,
            dst_ref=parts.at[me],
            send_sem=r_send,
            recv_sem=r_recv,
            device_id=(chip_s * 2 + c, to_p),
            device_id_type=MESH,
        ).start()

    def elsewhere(chip):
        return (xs[0] != chip[0]) | (ys[0] != chip[1]) | (zs[0] != chip[2])

    corner = acc[0:32, 0:32] + gram_of(*halves(cols, mean, 32))
    corner = jnp.concatenate([corner, jnp.zeros((32, 96), jnp.float32)], axis=1)
    tile = packed([corner[8 * i : 8 * i + 8] for i in range(4)])[0]
    lead[0] = tile[0:4]
    lead[1] = tile[4:8]

    @pl.when(elsewhere(LEAD))
    def _():
        for c in (1, 0):
            send_to(lead.at[c], 0, 0, c)

    acc[...] += gram_of(*halves(cols, mean))

    def pack_rows(t, carry):
        for half in range(2):
            v = [
                acc[pl.ds(pl.multiple_of(t * 32 + i * 8, 8), 8), half * 128 : half * 128 + 128] for i in range(4)
            ]
            for y, tile in enumerate(packed(v)):
                pack[0, t * 8 + half * 4 + y] = tile[0:4]
                pack[1, t * 8 + half * 4 + y] = tile[4:8]
        return carry

    lax.fori_loop(0, SAMP // 2, pack_rows, 0, unroll=True)

    for x, y, z in EARLY:
        @pl.when(elsewhere((x, y, z)))
        def _():
            chip_s, to_p = x * 2 + z // 2, (z % 2) * 4 + y
            for c in (1, 0):
                send_to(pack.at[c, chip_s * PAR + to_p], chip_s, to_p, c)

    def send_other(dx, dy, dz, dc):
        chip_s, to_p = xs[dx] * 2 + zs_high[dz], zs_low[dz] * 4 + ys[dy]
        send_to(pack.at[cores[dc], chip_s * PAR + to_p], chip_s, to_p, cores[dc])

    for dx, dy, dz, dc in OTHERS:
        if dx + dy + dz == 0:
            send_other(dx, dy, dz, dc)
        else:
            pl.when(is_later(xs[dx], ys[dy], zs[dz]))(functools.partial(send_other, dx, dy, dz, dc))

    parts[me] = pack[cores[0], (xs[0] * 2 + highs[0]) * PAR + par]

    got = parts.at[pl.ds(0, SAMP * PAR - 1)]
    pltpu.make_async_copy(got, got, r_recv).wait()
    total = parts[...]
    while total.shape[0] > 1:
        half = total.shape[0] // 2
        total = total[:half] + total[half:]
    tile = total[0]
    row = samp * ROWS + lax.broadcasted_iota(jnp.int32, (4, 32), 0)
    col = par * 32 + lax.broadcasted_iota(jnp.int32, (4, 32), 1)
    for g in range(4):
        shift = jnp.where(row + 4 * g == col, diag_shift, 0.0)
        o_ref[4 * g : 4 * g + 4, :] = tile[:, 32 * g : 32 * g + 32] / TOTAL + shift

    pltpu.make_async_copy(got, got, r_send).wait()
    sent = full.at[pl.ds(0, TOTAL - ROWS), :]
    pltpu.make_async_copy(sent, sent, a_send).wait()


def body(log_derivs):
    share = log_derivs.shape[1] // SAMP
    return pl.pallas_call(
        kernel,
        out_shape=jax.ShapeDtypeStruct((ROWS, TOTAL // PAR), jnp.float32),
        in_specs=[pl.BlockSpec(memory_space=pl.ANY)],
        out_specs=pl.BlockSpec(memory_space=pltpu.VMEM),
        scratch_shapes=[
            pltpu.VMEM((TOTAL, share), jnp.float32),
            pltpu.VMEM((TOTAL, TOTAL), jnp.float32),
            pltpu.VMEM((2, 4, 128), jnp.float32),
            pltpu.VMEM((2, SAMP * PAR // 2, 4, 128), jnp.float32),
            pltpu.VMEM((SAMP * PAR, 4, 128), jnp.float32),
            pltpu.SemaphoreType.DMA,
            pltpu.SemaphoreType.DMA,
            pltpu.SemaphoreType.DMA((CHUNKS,)),
            pltpu.SemaphoreType.DMA,
            pltpu.SemaphoreType.DMA,
        ],
        compiler_params=pltpu.CompilerParams(
            collective_id=0, has_side_effects=True, vmem_limit_bytes=60 * 1024 * 1024
        ),
        cost_estimate=pl.CostEstimate(flops=3 * 2 * TOTAL * TOTAL * share, bytes_accessed=2 << 20, transcendentals=0),
        name="sample_kernel",
    )(log_derivs)


def solution(mesh):
    return jax.shard_map(
        body,
        mesh=mesh,
        in_specs=(P("samp", "par"),),
        out_specs=P("samp", "par"),
        check_vma=False,
    )
```

```python
import functools

import jax
import jax.numpy as jnp
from jax import lax
from jax.experimental import pallas as pl
from jax.experimental.pallas import tpu as pltpu
from jax.sharding import PartitionSpec as P

diag_shift = 0.01
MESH = pl.DeviceIdType.MESH

ROWS = 16
SAMP = 16
PAR = 8
TOTAL = ROWS * SAMP
CHUNKS = 4

PARTNERS = [
    (2, 1, 0), (2, 1, 1), (1, 1, 0), (3, 1, 0), (1, 1, 1), (3, 1, 1), (2, 0, 0), (2, 0, 1),
    (0, 1, 0), (0, 1, 1), (1, 0, 0), (3, 0, 0), (1, 0, 1), (3, 0, 1), (0, 0, 1),
]


LEAD = (0, 0, 0)
EARLY = [(3, 0, 0), (1, 0, 0), (2, 0, 0), (0, 1, 0), (0, 0, 1)]


def is_later(x, y, z):
    return (y + z > 0) & (x + y + z != 1)


def turns(value, size):
    return [value] + [jnp.where(value + d < size, value + d, value + d - size) for d in range(1, size)]


def ring_distance(delta):
    return min(delta, 4 - delta)


OTHERS = sorted(
    [(a, b, c, d) for a in range(4) for b in range(4) for c in range(4) for d in range(2) if a + b + c + d > 0],
    key=lambda k: -3 * sum(ring_distance(i) for i in k[:3]) - k[3],
)


def kernel(x_ref, o_ref, full, acc, lead, pack, parts, local_sem, a_send, a_recv, r_send, r_recv):
    samp, par = lax.axis_index("samp"), lax.axis_index("par")
    share = full.shape[1]
    width = share // CHUNKS

    xs, highs, cores = turns(lax.div(samp, 4), 4), turns(lax.rem(lax.div(samp, 2), 2), 2), turns(lax.rem(samp, 2), 2)
    lows, ys = turns(lax.div(par, 4), 2), turns(lax.rem(par, 4), 4)
    partners = [xs[dx] * 4 + highs[dz] * 2 + cores[dc] for dx, dz, dc in PARTNERS]
    par_mates = [lows[dz] * 4 + ys[dy] for dz in range(2) for dy in range(4) if dz + dy > 0]

    barrier = pltpu.get_barrier_semaphore()
    for to in partners:
        pl.semaphore_signal(barrier, inc=1, device_id=(to, par), device_id_type=MESH)
    for to in par_mates:
        pl.semaphore_signal(barrier, inc=1, device_id=(samp, to), device_id_type=MESH)

    own = pl.ds(pl.multiple_of(samp * ROWS, ROWS), ROWS)
    keep = pltpu.make_async_copy(
        x_ref.at[:, pl.ds(pl.multiple_of(samp * share, share), share)], full.at[own, :], local_sem
    )
    keep.start()
    acc[...] = jnp.zeros_like(acc)
    pl.semaphore_wait(barrier, SAMP + PAR - 2)

    def send_chunk(k, carry):
        for to in partners:
            pltpu.make_async_remote_copy(
                src_ref=x_ref.at[:, pl.ds(pl.multiple_of(to * share + k * width, width), width)],
                dst_ref=full.at[own, pl.ds(pl.multiple_of(k * width, width), width)],
                send_sem=a_send,
                recv_sem=a_recv.at[k],
                device_id=(to, par),
                device_id_type=MESH,
            ).start()
        return carry

    lax.fori_loop(0, CHUNKS, send_chunk, 0)
    keep.wait()

    def dot(a, b):
        return lax.dot_general(a, b, (((1,), (1,)), ((), ())), preferred_element_type=jnp.float32)

    def arrived(k):
        cols = pl.ds(pl.multiple_of(k * width, width), width)
        got = full.at[pl.ds(0, TOTAL - ROWS), cols]
        pltpu.make_async_copy(got, got, a_recv.at[k]).wait()
        return cols, jnp.sum(full[:, cols], axis=0, keepdims=True) / TOTAL

    def halves(cols, mean, rows=TOTAL):
        block = full[:rows, cols] - mean
        high = block.astype(jnp.bfloat16)
        return high, (block - high.astype(jnp.float32)).astype(jnp.bfloat16)

    def gram_of(high, low):
        return dot(high, high) + (dot(high, low) + dot(low, high))

    def gram_chunk(k, carry):
        acc[...] += gram_of(*halves(*arrived(k)))
        return carry

    lane = lax.broadcasted_iota(jnp.int32, (8, 128), 1)
    top = lax.broadcasted_iota(jnp.int32, (8, 128), 0) < 4
    even, left = (lane // 32) % 2 == 0, lane < 64

    def packed(v):
        u = []
        for h in range(2):
            u.append(jnp.where(top, v[h], pltpu.roll(v[2 + h], 4, 0)))
            u.append(jnp.where(top, pltpu.roll(v[h], 4, 0), v[2 + h]))
        w = [[None, None], [None, None]]
        for a in range(2):
            w[a][0] = jnp.where(even, u[2 * a], pltpu.roll(u[2 * a + 1], 32, 1))
            w[a][1] = jnp.where(even, pltpu.roll(u[2 * a], 96, 1), u[2 * a + 1])
        tiles = []
        for b in range(2):
            for y0 in range(2):
                if b == 0:
                    tiles.append(jnp.where(left, w[0][y0], pltpu.roll(w[1][y0], 64, 1)))
                else:
                    tiles.append(jnp.where(left, pltpu.roll(w[0][y0], 64, 1), w[1][y0]))
        return tiles

    lax.fori_loop(0, CHUNKS - 1, gram_chunk, 0)
    cols, mean = arrived(CHUNKS - 1)

    me = samp * PAR + par
    zs = turns(highs[0] * 2 + lows[0], 4)
    zs_high = [lax.div(v, 2) for v in zs]
    zs_low = [v - 2 * h for v, h in zip(zs, zs_high)]

    def send_to(src, chip_s, to_p, c):
        pltpu.make_async_remote_copy(
            src_ref=src,
            dst_ref=parts.at[me],
            send_sem=r_send,
            recv_sem=r_recv,
            device_id=(chip_s * 2 + c, to_p),
            device_id_type=MESH,
        ).start()

    def elsewhere(chip):
        return (xs[0] != chip[0]) | (ys[0] != chip[1]) | (zs[0] != chip[2])

    corner = acc[0:32, 0:32] + gram_of(*halves(cols, mean, 32))
    corner = jnp.concatenate([corner, jnp.zeros((32, 96), jnp.float32)], axis=1)
    tile = packed([corner[8 * i : 8 * i + 8] for i in range(4)])[0]
    lead[0] = tile[0:4]
    lead[1] = tile[4:8]

    @pl.when(elsewhere(LEAD))
    def _():
        for c in (1, 0):
            send_to(lead.at[c], 0, 0, c)

    acc[...] += gram_of(*halves(cols, mean))

    def pack_rows(t, carry):
        for half in range(2):
            v = [
                acc[pl.ds(t * 32 + i * 8, 8), half * 128 : half * 128 + 128] for i in range(4)
            ]
            for y, tile in enumerate(packed(v)):
                pack[0, t * 8 + half * 4 + y] = tile[0:4]
                pack[1, t * 8 + half * 4 + y] = tile[4:8]
        return carry

    soon = sorted({x * 2 + z // 2 for x, y, z in EARLY})
    for t in soon:
        pack_rows(t, 0)

    for x, y, z in EARLY:
        @pl.when(elsewhere((x, y, z)))
        def _():
            chip_s, to_p = x * 2 + z // 2, (z % 2) * 4 + y
            for c in (1, 0):
                send_to(pack.at[c, chip_s * PAR + to_p], chip_s, to_p, c)

    for t in range(SAMP // 2):
        if t not in soon:
            pack_rows(t, 0)

    def send_other(dx, dy, dz, dc):
        chip_s, to_p = xs[dx] * 2 + zs_high[dz], zs_low[dz] * 4 + ys[dy]
        send_to(pack.at[cores[dc], chip_s * PAR + to_p], chip_s, to_p, cores[dc])

    for dx, dy, dz, dc in OTHERS:
        if dx + dy + dz == 0:
            send_other(dx, dy, dz, dc)
        else:
            pl.when(is_later(xs[dx], ys[dy], zs[dz]))(functools.partial(send_other, dx, dy, dz, dc))

    parts[me] = pack[cores[0], (xs[0] * 2 + highs[0]) * PAR + par]

    got = parts.at[pl.ds(0, SAMP * PAR - 1)]
    pltpu.make_async_copy(got, got, r_recv).wait()
    total = parts[...]
    while total.shape[0] > 1:
        half = total.shape[0] // 2
        total = total[:half] + total[half:]
    tile = total[0]
    row = samp * ROWS + lax.broadcasted_iota(jnp.int32, (4, 32), 0)
    col = par * 32 + lax.broadcasted_iota(jnp.int32, (4, 32), 1)
    for g in range(4):
        shift = jnp.where(row + 4 * g == col, diag_shift, 0.0)
        o_ref[4 * g : 4 * g + 4, :] = tile[:, 32 * g : 32 * g + 32] / TOTAL + shift

    pltpu.make_async_copy(got, got, r_send).wait()
    sent = full.at[pl.ds(0, TOTAL - ROWS), :]
    pltpu.make_async_copy(sent, sent, a_send).wait()


def body(log_derivs):
    share = log_derivs.shape[1] // SAMP
    return pl.pallas_call(
        kernel,
        out_shape=jax.ShapeDtypeStruct((ROWS, TOTAL // PAR), jnp.float32),
        in_specs=[pl.BlockSpec(memory_space=pl.ANY)],
        out_specs=pl.BlockSpec(memory_space=pltpu.VMEM),
        scratch_shapes=[
            pltpu.VMEM((TOTAL, share), jnp.float32),
            pltpu.VMEM((TOTAL, TOTAL), jnp.float32),
            pltpu.VMEM((2, 4, 128), jnp.float32),
            pltpu.VMEM((2, SAMP * PAR // 2, 4, 128), jnp.float32),
            pltpu.VMEM((SAMP * PAR, 4, 128), jnp.float32),
            pltpu.SemaphoreType.DMA,
            pltpu.SemaphoreType.DMA,
            pltpu.SemaphoreType.DMA((CHUNKS,)),
            pltpu.SemaphoreType.DMA,
            pltpu.SemaphoreType.DMA,
        ],
        compiler_params=pltpu.CompilerParams(
            collective_id=0, has_side_effects=True, vmem_limit_bytes=60 * 1024 * 1024
        ),
        cost_estimate=pl.CostEstimate(flops=3 * 2 * TOTAL * TOTAL * share, bytes_accessed=2 << 20, transcendentals=0),
        name="sample_kernel",
    )(log_derivs)


def solution(mesh):
    return jax.shard_map(
        body,
        mesh=mesh,
        in_specs=(P("samp", "par"),),
        out_specs=P("samp", "par"),
        check_vma=False,
    )
```
